32 devices in a mesh: dp: 8 (over z, x), tensor: 4 (over y, core).
Axes of the slice: x: 2, y: 2, z: 4, core: 2. Of those that a mesh axis runs over, the one named last changes fastest.
Arguments:
- frames: bfloat16 [4096, 768], P(('dp', 'tensor')), may hold values from -6 to 6
- clip_offsets: int32 [6], replicated, may hold values from 0 to 4095, as said below
- qkv_weight: bfloat16 [1, 768, 3, 768], P(None, 'dp', None, 'tensor'), may hold values from -0.3125 to 0.3125
- out_weight: bfloat16 [1, 768, 768], P(None, 'tensor', 'dp'), may hold values from -1.25 to 1.25
- up_weight: bfloat16 [1, 768, 3072], P(None, 'dp', 'tensor'), may hold values from -0.21875 to 0.21875
- down_weight: bfloat16 [1, 3072, 768], P(None, 'tensor', 'dp'), may hold values from -0.15625 to 0.15625
- ln_gain: float32 [1, 2, 768], replicated, may hold values from 0.1 to 1.9
- ln_bias: float32 [1, 2, 768], replicated, may hold values from -1.8 to 1.8
- proj_bias: float32 [1, 4, 768], replicated, may hold values from -1.8 to 1.8
- fc_bias: float32 [1, 3072], replicated, may hold values from -3 to 3
- out_cotangent: bfloat16 [4096, 768], P(('dp', 'tensor')), may hold values from -6 to 6
Outputs:
- encoded: bfloat16 [4096, 768], P(('dp', 'tensor'))
- frames_grad: bfloat16 [4096, 768], P(('dp', 'tensor'))
- qkv_grad: float32 [1, 768, 3, 768], P(None, 'dp', None, 'tensor')
- out_grad: float32 [1, 768, 768], P(None, 'tensor', 'dp')
- up_grad: float32 [1, 768, 3072], P(None, 'dp', 'tensor')
- down_grad: float32 [1, 3072, 768], P(None, 'tensor', 'dp')
- ln_gain_grad: float32 [1, 2, 768], replicated
- ln_bias_grad: float32 [1, 2, 768], replicated
- proj_bias_grad: float32 [1, 4, 768], replicated
- fc_bias_grad: float32 [1, 3072], replicated
The draws below stay inside these ranges and needn't reach their ends.
Inputs may be any that keep to these rules, and one draw needn't show every extreme that they name: clip_offsets[0] is 0 and the offsets rise; a clip runs from its offset up to the next one (the last up to 4096), holds at most 1500 frames, and some clip holds exactly 1500.
All inputs are finite; a program needn't handle non-finite values.
Results may differ from the reference program's by a relative error of at most 0.014.
The reference program's roundings to bfloat16 on the way count: a program that leaves them out, or rounds other values in their place, can miss the bound.
Values may be sent and summed in bfloat16 or wider, within the bound.
A program may use at most 128 MiB of HBM per device.

```python
import jax
import jax.numpy as jnp
from jax import lax

D = 768
HEADS = 12
HEAD = 64
FF = 3072
LAYERS = 1
CLIP = 1500
GROUP = 512
TOKENS = 4096
REACH = 3
NCLIPS = 6
N_DP = 8


def draw_clip_offsets(key, part):
    key = jax.random.fold_in(key, 7)
    clip_count = NCLIPS
    others_count = clip_count - 1
    remaining = TOKENS - CLIP
    base_len = remaining // others_count
    extra_count = remaining - base_len * others_count
    spread_max = max(min(base_len - 1, CLIP - base_len - 2), 1)
    pair_count = others_count // 2
    key_deltas = jax.random.fold_in(key, 1)
    key_signs = jax.random.fold_in(key, 2)
    key_order = jax.random.fold_in(key, 3)
    deltas = jax.random.randint(key_deltas, (pair_count,), 1, spread_max + 1, dtype=jnp.int32)
    signs = 2 * jax.random.randint(key_signs, (pair_count,), 0, 2, dtype=jnp.int32) - 1
    deltas = deltas * signs
    signed_deltas = jnp.concatenate([deltas, -deltas, jnp.zeros((others_count - 2 * pair_count,), jnp.int32)])
    lengths = base_len + (jnp.arange(others_count, dtype=jnp.int32) < extra_count).astype(jnp.int32) + signed_deltas
    lengths = jnp.concatenate([lengths, jnp.full((1,), CLIP, jnp.int32)])
    ordering = jax.random.permutation(key_order, clip_count)
    lengths = lengths[ordering].astype(jnp.int32)
    offsets = jnp.cumsum(lengths) - lengths
    return offsets.astype(jnp.int32)


def steps_of(stream_key, dims, split, least, high):
    level, own = 1.0, jax.random.fold_in(stream_key, 6)
    for position, blocks in split:
        draws = jnp.exp(jax.random.uniform(jax.random.fold_in(own, position), (blocks,), jnp.float32, least / len(split), high / len(split)))
        level = level * jnp.repeat(draws, dims[position] // blocks).reshape([-1 if axis == position else 1 for axis in range(len(dims))])
    return level


def gaussian(stream_key, shape, width, bound, shards=(), kind=jnp.bfloat16):
    entries = width * jax.random.normal(stream_key, shape, jnp.float32)
    if shards:
        entries = entries * steps_of(stream_key, shape, shards, -0.22, 0.18)
    return jnp.clip(entries, -bound, bound).astype(kind)


def setup_inputs(seed: int = 0) -> dict:
    arg_keys = jax.random.split(jax.random.key(seed), 12)
    frames = gaussian(arg_keys[0], (TOKENS, D), 1.0, 6.0, ((0, 32),))
    clip_offsets = draw_clip_offsets(jax.random.fold_in(arg_keys[11], 71), 0)
    qkv_weight = gaussian(arg_keys[2], (LAYERS, D, 3, D), (D // 2) ** -0.5, 0.3125, ((1, 8), (3, 4)))
    out_weight = gaussian(arg_keys[3], (LAYERS, D, D), (D // 32) ** -0.5, 1.25, ((1, 4), (2, 8)))
    up_weight = gaussian(arg_keys[4], (LAYERS, D, FF), D ** -0.5, 0.21875, ((1, 8), (2, 4)))
    down_weight = gaussian(arg_keys[5], (LAYERS, FF, D), (FF // 2) ** -0.5, 0.15625, ((1, 4), (2, 8)))
    ln_gain = jnp.clip(1.0 + 0.18 * jax.random.normal(arg_keys[6], (LAYERS, 2, D), jnp.float32), 0.1, 1.9)
    ln_bias = gaussian(arg_keys[7], (LAYERS, 2, D), 0.3, 1.8, (), jnp.float32)
    proj_bias = gaussian(arg_keys[8], (LAYERS, 4, D), 0.3, 1.8, (), jnp.float32)
    fc_bias = gaussian(arg_keys[9], (LAYERS, FF), 0.5, 3.0, (), jnp.float32)
    out_cotangent = gaussian(arg_keys[10], (TOKENS, D), 1.0, 6.0, ((0, 32),))
    return {"frames": frames, "clip_offsets": clip_offsets, "qkv_weight": qkv_weight, "out_weight": out_weight, "up_weight": up_weight, "down_weight": down_weight, "ln_gain": ln_gain, "ln_bias": ln_bias, "proj_bias": proj_bias, "fc_bias": fc_bias, "out_cotangent": out_cotangent}


EPSILON = 1e-05
HIGHEST = lax.Precision.HIGHEST

@jax.custom_vjp
def low(v):
    return lax.optimization_barrier(v.astype(jnp.bfloat16)).astype(jnp.float32)

@jax.custom_vjp
def low_back(v):
    return v

def low_keep(v):
    return (low(v), None)

def low_pass(kept, grad):
    return (grad,)

def back_keep(v):
    return (v, None)

def back_low(kept, grad):
    return (low(grad),)
low.defvjp(low_keep, low_pass)
low_back.defvjp(back_keep, back_low)

def norm_rows(values, gains, shifts):
    average = lax.optimization_barrier(jnp.mean(values, axis=-1, keepdims=True))
    centered = values - average
    variance = lax.optimization_barrier(jnp.mean(centered * centered, axis=-1, keepdims=True))
    return centered * lax.rsqrt(variance + EPSILON) * gains + shifts

def clip_ids(positions, clip_offsets):
    return lax.optimization_barrier(jnp.sum((positions[:, None] >= clip_offsets[None, :]).astype(jnp.int32), axis=1)) - 1

def attend_block(block_at, queries, keys_pad, values_pad, clip_offsets):
    window = (2 * REACH + 1) * GROUP
    first_row = block_at * GROUP
    query_block = lax.dynamic_slice_in_dim(queries, first_row, GROUP, 0)
    key_window = lax.dynamic_slice_in_dim(keys_pad, first_row, window, 0)
    value_window = lax.dynamic_slice_in_dim(values_pad, first_row, window, 0)
    query_pos = first_row + jnp.arange(GROUP, dtype=jnp.int32)
    key_pos = first_row - REACH * GROUP + jnp.arange(window, dtype=jnp.int32)
    allowed = clip_ids(query_pos, clip_offsets)[:, None] == clip_ids(key_pos, clip_offsets)[None, :]
    allowed = allowed & (key_pos >= 0)[None, :] & (key_pos < TOKENS)[None, :]
    scores = jnp.einsum('qhd,khd->hqk', query_block, key_window, precision=HIGHEST) * HEAD ** (-0.5)
    scores = low_back(scores)
    masked = jnp.where(allowed[None], scores, -1000000000.0)
    largest = lax.optimization_barrier(jnp.max(masked, axis=-1, keepdims=True))
    weights = jnp.exp(masked - largest)
    attn_probs = low(weights / lax.optimization_barrier(jnp.sum(weights, axis=-1, keepdims=True)))
    return jnp.einsum('hqk,khd->qhd', attn_probs, value_window, precision=HIGHEST)

def encoder_layer(state, layer_idx, qkv_all, out_all, up_all, down_all, gain_all, shift_all, pbias_all, fbias_all, clip_offsets):
    normed = low(norm_rows(state, gain_all[layer_idx, 0], shift_all[layer_idx, 0]))
    zeros_row = jnp.zeros_like(pbias_all[layer_idx, 0])
    bias_rows = jnp.stack([pbias_all[layer_idx, 0], zeros_row, pbias_all[layer_idx, 1]])
    projected = jnp.einsum('nd,dkh->nkh', normed, qkv_all[layer_idx], precision=HIGHEST) + bias_rows[None]
    projected = low(low_back(projected))
    queries = projected[:, 0].reshape(TOKENS, HEADS, HEAD)
    all_keys = projected[:, 1].reshape(TOKENS, HEADS, HEAD)
    values = projected[:, 2].reshape(TOKENS, HEADS, HEAD)
    padding = ((REACH * GROUP, REACH * GROUP), (0, 0), (0, 0))
    keys_pad = jnp.pad(all_keys, padding)
    values_pad = jnp.pad(values, padding)
    block_fn = jax.checkpoint(attend_block)
    attended = lax.map(lambda block_at: block_fn(block_at, queries, keys_pad, values_pad, clip_offsets), jnp.arange(N_DP, dtype=jnp.int32))
    attended = low(low_back(attended.reshape(TOKENS, D)))
    branch = low_back(jnp.dot(attended, out_all[layer_idx], precision=HIGHEST) + pbias_all[layer_idx, 2])
    hidden = state + branch
    normed_two = low(norm_rows(hidden, gain_all[layer_idx, 1], shift_all[layer_idx, 1]))
    upper = low_back(jnp.dot(normed_two, up_all[layer_idx], precision=HIGHEST) + fbias_all[layer_idx])
    activated = low(jax.nn.gelu(upper, approximate=False))
    branch_two = low_back(jnp.dot(activated, down_all[layer_idx], precision=HIGHEST) + pbias_all[layer_idx, 3])
    return hidden + branch_two

def reference(frames, clip_offsets, qkv_weight, out_weight, up_weight, down_weight, ln_gain, ln_bias, proj_bias, fc_bias, out_cotangent):

    def forward(state, qkv_all, out_all, up_all, down_all, gain_all, shift_all, pbias_all, fbias_all):
        for layer_idx in range(LAYERS):
            state = encoder_layer(state, layer_idx, qkv_all, out_all, up_all, down_all, gain_all, shift_all, pbias_all, fbias_all, clip_offsets)
        return state
    encoded, pullback = jax.vjp(forward, frames.astype(jnp.float32), qkv_weight.astype(jnp.float32), out_weight.astype(jnp.float32), up_weight.astype(jnp.float32), down_weight.astype(jnp.float32), ln_gain, ln_bias, proj_bias, fc_bias)
    grads = pullback(out_cotangent.astype(jnp.float32))
    return (encoded.astype(jnp.bfloat16), grads[0].astype(jnp.bfloat16), grads[1], grads[2], grads[3], grads[4], grads[5], grads[6], grads[7], grads[8])
```

```python
from functools import partial

import jax
import jax.numpy as jnp
from jax import lax
from jax.experimental import pallas as pl
from jax.experimental.pallas import tpu as pltpu
from jax.sharding import PartitionSpec as P

D = 768
HEAD = 64
REACH = 3
EPSILON = 1e-05
MESH = pl.DeviceIdType.MESH
F32 = jnp.float32
BF16 = jnp.bfloat16
VMEM = pl.BlockSpec(memory_space=pltpu.VMEM)
LIMIT = 56 * 1024 * 1024


def dma(n):
    return pltpu.SemaphoreType.DMA((n,))


def send(src, dst, send_sem, recv_sem, where):
    return pltpu.make_async_remote_copy(
        src_ref=src, dst_ref=dst, send_sem=send_sem, recv_sem=recv_sem,
        device_id=where, device_id_type=MESH,
    )


class Place:
    def __init__(self, sizes):
        self.n, self.t_count = sizes
        self.half = self.n // 2
        self.dp = lax.axis_index("dp")
        self.t = lax.axis_index("tensor")
        self.hi = lax.div(self.dp, 2)
        self.lo = lax.rem(self.dp, 2)

    def tensor_at(self, k):
        return lax.rem(self.t + k, self.t_count)

    def tensor_back(self, k):
        return lax.rem(self.t + self.t_count - k, self.t_count)

    def hi_at(self, k):
        return lax.rem(self.hi + k, self.half)

    def hi_back(self, k):
        return lax.rem(self.hi + self.half - k, self.half)

    def partner(self):
        return {"dp": self.hi * 2 + 1 - self.lo}

    def along(self, k):
        return {"dp": self.hi_at(k) * 2 + self.lo}


def greet(peers):
    barrier = pltpu.get_barrier_semaphore()
    for peer in peers:
        pl.semaphore_signal(barrier, inc=1, device_id=peer, device_id_type=MESH)
    pl.semaphore_wait(barrier, len(peers))


def tensor_peers(place):
    return [{"tensor": place.tensor_at(k)} for k in range(1, place.t_count)]


def two_level_peers(place):
    return [place.partner()] + [place.along(k) for k in range(1, place.half)]


def tensor_gather_start(place, src, group, ss, rs):
    copies = []
    for k in range(1, place.t_count):
        c = send(src, group.at[place.t], ss.at[k], rs.at[k], {"tensor": place.tensor_at(k)})
        c.start()
        copies.append(c)
    return copies


def tensor_scatter_start(place, part, slots, ss, rs):
    copies = []
    for k in range(1, place.t_count):
        c = send(part.at[place.tensor_at(k)], slots.at[k - 1], ss.at[k], rs.at[k],
                 {"tensor": place.tensor_at(k)})
        c.start()
        copies.append(c)
    return copies


def tensor_scatter_sum(place, part, slots, copies):
    total = part[place.t].astype(F32)
    for k in range(1, place.t_count):
        copies[k - 1].wait()
        total = total + slots[k - 1].astype(F32)
    return total


def gather_start(place, local, full, ss, rs, xs, xr):
    direct = [None]
    forwards = []
    mine = place.dp
    c = send(local, full.at[mine], xs.at[0], xr.at[0], place.partner())
    c.start()
    forwards.append(c)
    for k in range(1, place.half):
        c = send(local, full.at[mine], ss.at[k], rs.at[k], place.along(k))
        c.start()
        direct.append(c)
    return direct, forwards


def gather_finish(place, full, direct, forwards, xs, xr):
    for k in range(1, place.half):
        direct[k].wait_recv()
        got = full.at[place.hi_back(k) * 2 + place.lo]
        c = send(got, got, xs.at[k], xr.at[k], place.partner())
        c.start()
        forwards.append(c)
    for k in range(1, place.half):
        direct[k].wait_send()
    for c in forwards:
        c.wait()


def scatter_start(place, part, rx, xs, xr):
    copies = [None] * place.half
    for k in list(range(1, place.half)) + [0]:
        c = send(part.at[place.hi_at(k) * 2 + 1 - place.lo], rx.at[k], xs.at[k], xr.at[k],
                 place.partner())
        c.start()
        copies[k] = c
    return copies


def scatter_middle(place, part, rx, stage, rz, copies, ss, rs):
    onward = [None]
    for k in range(1, place.half):
        copies[k].wait()
        total = part[place.hi_at(k) * 2 + place.lo].astype(F32) + rx[k].astype(F32)
        stage[k] = total.astype(BF16)
        c = send(stage.at[k], rz.at[k], ss.at[k], rs.at[k], place.along(k))
        c.start()
        onward.append(c)
    copies[0].wait()
    return onward


def scatter_finish(place, part, rx, rz, onward, out):
    total = part[place.hi * 2 + place.lo].astype(F32) + rx[0].astype(F32)
    for k in range(1, place.half):
        onward[k].wait()
        total = total + rz[k].astype(F32)
    out[...] = total


def norm_parts(values):
    average = jnp.mean(values, axis=-1, keepdims=True)
    centered = values - average
    variance = jnp.mean(centered * centered, axis=-1, keepdims=True)
    r = lax.rsqrt(variance + EPSILON)
    return centered * r, r


def norm_back(xhat, r, grad, gain):
    e = grad * gain
    return r * (
        e - jnp.mean(e, axis=-1, keepdims=True)
        - xhat * jnp.mean(e * xhat, axis=-1, keepdims=True)
    )


def column_sum(values):
    return jnp.sum(values, axis=0, keepdims=True)


def open_kernel(sizes, frames, cot, weights, gain, shift, normed_g, cot_g, w_full,
                mine, ns, nr, cs, cr, ws, wr, xs, xr):
    place = Place(sizes)
    greet(tensor_peers(place) + two_level_peers(place))
    direct, forwards = gather_start(place, weights, w_full, ws, wr, xs, xr)
    cots = tensor_gather_start(place, cot, cot_g, cs, cr)
    xhat, _ = norm_parts(frames[...].astype(F32))
    mine[...] = (xhat * gain[...] + shift[...]).astype(BF16)
    normeds = tensor_gather_start(place, mine, normed_g, ns, nr)
    normed_g[place.t] = mine[...]
    cot_g[place.t] = cot[...]
    w_full[place.dp] = weights[...]
    gather_finish(place, w_full, direct, forwards, xs, xr)
    for c in cots + normeds:
        c.wait()


def near_kernel(sizes, kv, window, ss, rs):
    place = Place(sizes)
    n = place.n
    gaps = [g for g in (1, -1, 2, -2, 3, -3)]
    barrier = pltpu.get_barrier_semaphore()
    here = [(place.dp + g >= 0) & (place.dp + g < n) for g in gaps]
    for g, ok in zip(gaps, here):
        @pl.when(ok)
        def _(g=g):
            pl.semaphore_signal(barrier, inc=1, device_id={"dp": place.dp + g},
                                device_id_type=MESH)
    pl.semaphore_wait(barrier, sum(ok.astype(jnp.int32) for ok in here))

    def copy(i, g):
        return send(kv, window.at[REACH - g], ss.at[i], rs.at[i], {"dp": place.dp + g})

    for i, g in enumerate(gaps):
        @pl.when(here[i])
        def _(i=i, g=g):
            copy(i, g).start()
    window[REACH] = kv[...]
    for i, g in enumerate(gaps):
        @pl.when(jnp.logical_not((place.dp - g >= 0) & (place.dp - g < n)))
        def _(g=g):
            window[REACH - g] = jnp.zeros_like(kv)
    for i, g in enumerate(gaps):
        @pl.when(here[i])
        def _(i=i, g=g):
            copy(i, g).wait_send()

        @pl.when((place.dp - g >= 0) & (place.dp - g < n))
        def _(i=i, g=g):
            copy(i, g).wait_recv()


def middle_kernel(sizes, part, frames, gain, shift, bias, hidden, c_g,
                  slots, mine, ps, pr, cs, cr):
    place = Place(sizes)
    greet(tensor_peers(place))
    copies = tensor_scatter_start(place, part, slots, ps, pr)
    h = frames[...].astype(F32) + (tensor_scatter_sum(place, part, slots, copies) + bias[...])
    hidden[...] = h
    xhat, _ = norm_parts(h)
    mine[...] = (xhat * gain[...] + shift[...]).astype(BF16)
    sends = tensor_gather_start(place, mine, c_g, cs, cr)
    c_g[place.t] = mine[...]
    for c in sends:
        c.wait()


def turn_kernel(sizes, down, dc_part, hidden, cot, gain, bias, encoded, dh_out, dz_g, vec,
                slots_d, slots_c, mine, ds, dr, cs, cr, zs, zr):
    place = Place(sizes)
    greet(tensor_peers(place))
    c_copies = tensor_scatter_start(place, dc_part, slots_c, cs, cr)
    d_copies = tensor_scatter_start(place, down, slots_d, ds, dr)
    h = hidden[...]
    xhat, r = norm_parts(h)
    dc = tensor_scatter_sum(place, dc_part, slots_c, c_copies)
    dh = cot[...].astype(F32) + norm_back(xhat, r, dc, gain[...])
    dh_out[...] = dh
    dz = dh.astype(BF16)
    mine[...] = dz
    sends = tensor_gather_start(place, mine, dz_g, zs, zr)
    dz_g[place.t] = dz
    vec[0:1] = column_sum(dc * xhat)
    vec[1:2] = column_sum(dc)
    vec[2:3] = column_sum(dz.astype(F32))
    vec[3:4] = column_sum(cot[...].astype(F32))
    encoded[...] = (
        h + (tensor_scatter_sum(place, down, slots_d, d_copies) + bias[...])
    ).astype(BF16)
    for c in sends:
        c.wait()


def back_kernel(sizes, dkv, grads, dkv_out, grads_out,
                slots, rx, stage, rz, ks, kr, xs, xr, ss, rs):
    place = Place(sizes)
    n = place.n
    gaps = [g for g in (1, -1, 2, -2, 3, -3)]

    def inside(g):
        return (place.dp + g >= 0) & (place.dp + g < n)

    peers = two_level_peers(place)
    barrier = pltpu.get_barrier_semaphore()
    for peer in peers:
        pl.semaphore_signal(barrier, inc=1, device_id=peer, device_id_type=MESH)
    for g in gaps:
        @pl.when(inside(g))
        def _(g=g):
            pl.semaphore_signal(barrier, inc=1, device_id={"dp": place.dp + g},
                                device_id_type=MESH)
    pl.semaphore_wait(barrier, len(peers) + sum(inside(g).astype(jnp.int32) for g in gaps))

    def copy(i, g):
        return send(dkv.at[REACH + g], slots.at[i], ks.at[i], kr.at[i], {"dp": place.dp + g})

    for i, g in enumerate(gaps):
        @pl.when(inside(g))
        def _(i=i, g=g):
            copy(i, g).start()
    copies = scatter_start(place, grads, rx, xs, xr)
    dkv_out[...] = dkv[REACH].astype(F32)
    onward = scatter_middle(place, grads, rx, stage, rz, copies, ss, rs)
    for i, g in enumerate(gaps):
        @pl.when(inside(g))
        def _(i=i, g=g):
            copy(i, g).wait_send()

        @pl.when(inside(-g))
        def _(i=i, g=g):
            copy(i, g).wait_recv()
            dkv_out[...] += slots[i].astype(F32)
    scatter_finish(place, grads, rx, rz, onward, grads_out)


def close_kernel(sizes, da_part, frames, dh, gain, grads, vec_in, frames_grad, grads_out, vec_out,
                 slots, rx, stage, rz, vec, vt, vsum, vx, vpair, vz,
                 ps, pr, xs, xr, ss, rs, vs, vr, us, ur, zs, zr):
    place = Place(sizes)
    greet(tensor_peers(place) + two_level_peers(place))
    copies = tensor_scatter_start(place, da_part, slots, ps, pr)
    x_copies = scatter_start(place, grads, rx, xs, xr)
    xhat, r = norm_parts(frames[...].astype(F32))
    da = tensor_scatter_sum(place, da_part, slots, copies)
    frames_grad[...] = (dh[...] + norm_back(xhat, r, da, gain[...])).astype(BF16)
    vec[...] = vec_in[...]
    vec[0:1] = column_sum(da * xhat)
    vec[2:3] = column_sum(da)
    v_copies = []
    for k in range(1, place.t_count):
        c = send(vec, vt.at[k - 1], vs.at[k], vr.at[k], {"tensor": place.tensor_at(k)})
        c.start()
        v_copies.append(c)
    onward = scatter_middle(place, grads, rx, stage, rz, x_copies, ss, rs)
    for c in v_copies:
        c.wait()
    vsum[place.t] = vec[...]
    for k in range(1, place.t_count):
        vsum[place.tensor_back(k)] = vt[k - 1]
    total = vsum[0]
    for k in range(1, place.t_count):
        total = total + vsum[k]
    vx[0] = total
    c = send(vx.at[0], vx.at[1], us.at[0], ur.at[0], place.partner())
    c.start()
    c.wait()
    vpair[...] = vx[0] + vx[1]
    vz[place.hi] = vpair[...]
    z_copies = []
    for k in range(1, place.half):
        c = send(vpair, vz.at[place.hi], zs.at[k], zr.at[k], place.along(k))
        c.start()
        z_copies.append(c)
    scatter_finish(place, grads, rx, rz, onward, grads_out)
    for c in z_copies:
        c.wait()
    total = vz[0]
    for k in range(1, place.half):
        total = total + vz[k]
    vec_out[...] = total


def call(kernel, sizes, ident, outs, scratch, *args):
    return pl.pallas_call(
        partial(kernel, sizes),
        out_shape=[jax.ShapeDtypeStruct(s, t) for s, t in outs],
        in_specs=[VMEM] * len(args),
        out_specs=[VMEM] * len(outs),
        scratch_shapes=scratch,
        compiler_params=pltpu.CompilerParams(
            collective_id=ident, has_side_effects=True, vmem_limit_bytes=LIMIT
        ),
    )(*args)


def clip_ids(positions, clip_offsets):
    return jnp.sum((positions[:, None] >= clip_offsets[None, :]).astype(jnp.int32), axis=1) - 1


def contract_rows(left, right):
    return lax.dot_general(
        left, right, (((0,), (0,)), ((), ())), preferred_element_type=jnp.float32
    )


def contract_cols(left, right):
    return lax.dot_general(
        left, right, (((1,), (1,)), ((), ())), preferred_element_type=jnp.float32
    )


def attention_mask(dp_idx, dp_count, group_rows, clip_offsets):
    window = (2 * REACH + 1) * group_rows
    query_pos = dp_idx * group_rows + jnp.arange(group_rows, dtype=jnp.int32)
    key_pos = (dp_idx - REACH) * group_rows + jnp.arange(window, dtype=jnp.int32)
    inside = (key_pos >= 0) & (key_pos < dp_count * group_rows)
    same_clip = (
        clip_ids(query_pos, clip_offsets)[:, None] == clip_ids(key_pos, clip_offsets)[None, :]
    )
    return same_clip & inside[None, :]


def head_scores(queries, all_keys, allowed):
    group_rows = queries.shape[0]
    heads_here = queries.shape[1] // HEAD
    scores = jnp.einsum(
        "qhd,khd->hqk",
        queries.reshape(group_rows, heads_here, HEAD),
        all_keys.reshape(all_keys.shape[0], heads_here, HEAD),
        preferred_element_type=jnp.float32,
    ) * HEAD ** (-0.5)
    return jnp.where(allowed[None], scores, -1000000000.0)


def attention_forward(queries, all_keys, values, allowed):
    group_rows, local_width = queries.shape
    heads_here = local_width // HEAD
    masked = head_scores(queries, all_keys, allowed)
    largest = jnp.max(masked, axis=-1, keepdims=True)
    weights = jnp.exp(masked - largest)
    totals = jnp.sum(weights, axis=-1, keepdims=True)
    attn_probs = (weights / totals).astype(BF16)
    log_total = largest + jnp.log(totals)
    attended = jnp.einsum(
        "hqk,khd->qhd", attn_probs, values.reshape(-1, heads_here, HEAD),
        preferred_element_type=F32,
    )
    return log_total, attended.reshape(group_rows, local_width).astype(BF16)


def attention_backward(grad_attended, queries, all_keys, values, allowed, log_total):
    group_rows = queries.shape[0]
    local_width = queries.shape[1]
    heads_here = local_width // HEAD
    head_scale = HEAD ** (-0.5)
    masked = head_scores(queries, all_keys, allowed)
    attn_probs = jnp.exp(masked - log_total)
    grad_heads = grad_attended.reshape(group_rows, heads_here, HEAD)
    grad_probs = jnp.einsum(
        "qhd,khd->hqk", grad_heads, values.reshape(-1, heads_here, HEAD),
        preferred_element_type=F32,
    )
    inner_sum = jnp.sum(attn_probs * grad_probs, axis=-1, keepdims=True)
    grad_scores = (attn_probs * (grad_probs - inner_sum)).astype(BF16)
    grad_queries = jnp.einsum(
        "hqk,khd->qhd", grad_scores, all_keys.reshape(-1, heads_here, HEAD),
        preferred_element_type=F32,
    ) * head_scale
    grad_keys = jnp.einsum(
        "hqk,qhd->khd", grad_scores, queries.reshape(group_rows, heads_here, HEAD),
        preferred_element_type=F32,
    ) * head_scale
    grad_values = jnp.einsum(
        "hqk,qhd->khd", attn_probs.astype(BF16), grad_heads, preferred_element_type=F32,
    )
    shape = (2 * REACH + 1, group_rows, local_width)
    dkv = jnp.concatenate(
        [grad_keys.astype(BF16).reshape(shape), grad_values.astype(BF16).reshape(shape)], axis=2
    )
    return grad_queries.reshape(group_rows, local_width).astype(BF16), dkv


def place_slice(piece, tensor_idx, full_width):
    return lax.dynamic_update_slice_in_dim(
        jnp.zeros((full_width,), F32), piece, tensor_idx * piece.shape[0], 0
    )


def shards(
    frames, clip_offsets, qkv_weight, out_weight, up_weight, down_weight,
    ln_gain, ln_bias, proj_bias, fc_bias, out_cotangent,
):
    t_idx = lax.axis_index("tensor")
    dp_idx = lax.axis_index("dp")
    n = lax.axis_size("dp")
    t_count = lax.axis_size("tensor")
    sizes = (n, t_count)
    half = n // 2
    rows = frames.shape[0]
    group = rows * t_count
    wrows = qkv_weight.shape[1]
    width = qkv_weight.shape[3]
    ff = up_weight.shape[2]
    ff_all = fc_bias.shape[1]
    gains, shifts, pbias, fbias = ln_gain[0], ln_bias[0], proj_bias[0], fc_bias[0]

    w_local = jnp.concatenate(
        [qkv_weight[0].reshape(wrows, 3 * width), out_weight[0].T, up_weight[0], down_weight[0].T],
        axis=1,
    )
    total = w_local.shape[1]
    t3 = (t_count, rows, D)
    normed_g, cot_g, w_full = call(
        open_kernel, sizes, 1,
        [(t3, BF16), (t3, BF16), ((n, wrows, total), BF16)],
        [pltpu.VMEM((rows, D), BF16), dma(t_count), dma(t_count), dma(t_count), dma(t_count),
         dma(half), dma(half), dma(half), dma(half)],
        frames, out_cotangent, w_local, gains[0:1], shifts[0:1],
    )
    normed_g = normed_g.reshape(group, D)
    cot_g = cot_g.reshape(group, D)
    w_full = w_full.reshape(D, total)
    cut = [3 * width, 4 * width, 4 * width + ff]
    qkv_full = w_full[:, :cut[0]]
    out_t = w_full[:, cut[0]:cut[1]]
    up_full = w_full[:, cut[1]:cut[2]]
    down_t = w_full[:, cut[2]:]

    allowed = attention_mask(dp_idx, n, group, clip_offsets)
    q_bias = lax.dynamic_slice_in_dim(pbias[0], t_idx * width, width)
    v_bias = lax.dynamic_slice_in_dim(pbias[1], t_idx * width, width)
    bias_row = jnp.concatenate([q_bias, jnp.zeros_like(q_bias), v_bias])
    projected = (jnp.dot(normed_g, qkv_full, preferred_element_type=F32) + bias_row).astype(BF16)
    queries = projected[:, :width]
    (window,) = call(
        near_kernel, sizes, 2, [((2 * REACH + 1, group, 2 * width), BF16)],
        [dma(6), dma(6)], projected[:, width:],
    )
    window = window.reshape(-1, 2 * width)
    all_keys, values = window[:, :width], window[:, width:]
    log_total, attended = attention_forward(queries, all_keys, values, allowed)

    part = contract_cols(attended, out_t).astype(BF16).reshape(t3)
    hidden, c_g = call(
        middle_kernel, sizes, 3, [((rows, D), F32), (t3, BF16)],
        [pltpu.VMEM((t_count - 1, rows, D), BF16), pltpu.VMEM((rows, D), BF16)]
        + [dma(t_count)] * 4,
        part, frames, gains[1:2], shifts[1:2], pbias[2:3],
    )
    c_g = c_g.reshape(group, D)
    upper = jnp.dot(c_g, up_full, preferred_element_type=F32)
    upper = upper + lax.dynamic_slice_in_dim(fbias, t_idx * ff, ff)
    cdf = 0.5 * (1.0 + lax.erf(upper * (2.0 ** -0.5)))
    activated = (upper * cdf).astype(BF16)
    down_part = contract_cols(activated, down_t).astype(BF16).reshape(t3)

    slope = cdf + upper * jnp.exp(-0.5 * upper * upper) * 0.3989422804014327
    grad_act = jnp.dot(cot_g, down_t, preferred_element_type=F32)
    grad_upper = (grad_act * slope).astype(BF16)
    dc_part = contract_cols(grad_upper, up_full).astype(BF16).reshape(t3)
    encoded, dh, dz_g, vec2 = call(
        turn_kernel, sizes, 4,
        [((rows, D), BF16), ((rows, D), F32), (t3, BF16), ((4, D), F32)],
        [pltpu.VMEM((t_count - 1, rows, D), BF16), pltpu.VMEM((t_count - 1, rows, D), BF16),
         pltpu.VMEM((rows, D), BF16)] + [dma(t_count)] * 6,
        down_part, dc_part, hidden, out_cotangent, gains[1:2], pbias[3:4],
    )
    dz_g = dz_g.reshape(group, D)
    fc_grad = place_slice(jnp.sum(grad_upper, axis=0, dtype=F32), t_idx, ff_all)
    down_grad_t = contract_rows(cot_g, activated)
    up_grad = contract_rows(c_g, grad_upper)
    out_grad_t = contract_rows(dz_g, attended)
    grad_attended = jnp.dot(dz_g, out_t, preferred_element_type=F32).astype(BF16)
    grad_queries, dkv = attention_backward(
        grad_attended, queries, all_keys, values, allowed, log_total
    )
    three = jnp.concatenate([out_grad_t, up_grad, down_grad_t], axis=1).astype(BF16)
    w3 = three.shape[1]
    dkv_sum, three = call(
        back_kernel, sizes, 5, [((group, 2 * width), F32), ((wrows, w3), F32)],
        [pltpu.VMEM((6, group, 2 * width), BF16)] + [pltpu.VMEM((half, wrows, w3), BF16)] * 3
        + [dma(6)] * 2 + [dma(half)] * 4,
        dkv, three.reshape(n, wrows, w3),
    )
    out_grad = three[:, :width].T
    up_grad = three[:, width:width + ff]
    down_grad = three[:, width + ff:].T

    grad_proj = jnp.concatenate([grad_queries, dkv_sum.astype(BF16)], axis=1)
    qkv_grad = contract_rows(normed_g, grad_proj).astype(BF16)
    bias_sums = jnp.sum(grad_proj, axis=0, dtype=F32)
    da_part = contract_cols(grad_proj, qkv_full).astype(BF16).reshape(t3)
    zero = jnp.zeros((1, D), F32)
    vec = jnp.concatenate([
        zero, vec2[0:1], zero, vec2[1:2],
        place_slice(bias_sums[:width], t_idx, D)[None],
        place_slice(bias_sums[2 * width:], t_idx, D)[None],
        vec2[2:4], fc_grad.reshape(-1, D), zero, zero, zero, zero,
    ], axis=0)
    vshape = vec.shape
    frames_grad, qkv_grad, vec = call(
        close_kernel, sizes, 6,
        [((rows, D), BF16), ((wrows, 3 * width), F32), (vshape, F32)],
        [pltpu.VMEM((t_count - 1, rows, D), BF16)]
        + [pltpu.VMEM((half, wrows, 3 * width), BF16)] * 3
        + [pltpu.VMEM(vshape, F32), pltpu.VMEM((t_count - 1,) + vshape, F32),
           pltpu.VMEM((t_count,) + vshape, F32), pltpu.VMEM((2,) + vshape, F32),
           pltpu.VMEM(vshape, F32), pltpu.VMEM((half,) + vshape, F32)]
        + [dma(t_count)] * 2 + [dma(half)] * 4 + [dma(t_count)] * 2 + [dma(1)] * 2
        + [dma(half)] * 2,
        da_part, frames, dh, gains[0:1], qkv_grad.reshape(n, wrows, 3 * width), vec,
    )
    fc_rows = ff_all // D
    return (
        encoded,
        frames_grad,
        qkv_grad.reshape(1, wrows, 3, width),
        out_grad[None],
        up_grad[None],
        down_grad[None],
        vec[None, 0:2],
        vec[None, 2:4],
        vec[None, 4:8],
        vec[8:8 + fc_rows].reshape(1, ff_all),
    )


def solution(mesh):
    return jax.shard_map(
        shards,
        mesh=mesh,
        in_specs=(
            P(("dp", "tensor"), None),
            P(),
            P(None, "dp", None, "tensor"),
            P(None, "tensor", "dp"),
            P(None, "dp", "tensor"),
            P(None, "tensor", "dp"),
            P(),
            P(),
            P(),
            P(),
            P(("dp", "tensor"), None),
        ),
        out_specs=(
            P(("dp", "tensor"), None),
            P(("dp", "tensor"), None),
            P(None, "dp", None, "tensor"),
            P(None, "tensor", "dp"),
            P(None, "dp", "tensor"),
            P(None, "tensor", "dp"),
            P(),
            P(),
            P(),
            P(),
        ),
        check_vma=False,
    )
```

```python
from functools import partial

import jax
import jax.numpy as jnp
from jax import lax
from jax.experimental import pallas as pl
from jax.experimental.pallas import tpu as pltpu
from jax.sharding import PartitionSpec as P

D = 768
HEAD = 64
REACH = 3
EPSILON = 1e-05
MESH = pl.DeviceIdType.MESH
F32 = jnp.float32
BF16 = jnp.bfloat16
VMEM = pl.BlockSpec(memory_space=pltpu.VMEM)
LIMIT = 56 * 1024 * 1024


def dma(n):
    return pltpu.SemaphoreType.DMA((n,))


def send(src, dst, send_sem, recv_sem, where):
    return pltpu.make_async_remote_copy(
        src_ref=src, dst_ref=dst, send_sem=send_sem, recv_sem=recv_sem,
        device_id=where, device_id_type=MESH,
    )


class Place:
    def __init__(self, sizes):
        self.n, self.t_count = sizes
        self.half = self.n // 2
        self.dp = lax.axis_index("dp")
        self.t = lax.axis_index("tensor")
        self.hi = lax.div(self.dp, 2)
        self.lo = lax.rem(self.dp, 2)

    def tensor_at(self, k):
        return lax.rem(self.t + k, self.t_count)

    def tensor_back(self, k):
        return lax.rem(self.t + self.t_count - k, self.t_count)

    def hi_at(self, k):
        return lax.rem(self.hi + k, self.half)

    def hi_back(self, k):
        return lax.rem(self.hi + self.half - k, self.half)

    def partner(self):
        return {"dp": self.hi * 2 + 1 - self.lo}

    def along(self, k):
        return {"dp": self.hi_at(k) * 2 + self.lo}


def greet(peers):
    barrier = pltpu.get_barrier_semaphore()
    for peer in peers:
        pl.semaphore_signal(barrier, inc=1, device_id=peer, device_id_type=MESH)
    pl.semaphore_wait(barrier, len(peers))


def tensor_peers(place):
    return [{"tensor": place.tensor_at(k)} for k in range(1, place.t_count)]


def two_level_peers(place):
    return [place.partner()] + [place.along(k) for k in range(1, place.half)]


def tensor_gather_start(place, src, group, ss, rs):
    copies = []
    for k in range(1, place.t_count):
        c = send(src, group.at[place.t], ss.at[k], rs.at[k], {"tensor": place.tensor_at(k)})
        c.start()
        copies.append(c)
    return copies


def tensor_scatter_start(place, part, slots, ss, rs):
    copies = []
    for k in range(1, place.t_count):
        c = send(part.at[place.tensor_at(k)], slots.at[k - 1], ss.at[k], rs.at[k],
                 {"tensor": place.tensor_at(k)})
        c.start()
        copies.append(c)
    return copies


def tensor_scatter_sum(place, part, slots, copies):
    total = part[place.t].astype(F32)
    for k in range(1, place.t_count):
        copies[k - 1].wait()
        total = total + slots[k - 1].astype(F32)
    return total


def gather_start(place, local, full, ss, rs, xs, xr):
    direct = [None]
    forwards = []
    mine = place.dp
    c = send(local, full.at[mine], xs.at[0], xr.at[0], place.partner())
    c.start()
    forwards.append(c)
    for k in range(1, place.half):
        c = send(local, full.at[mine], ss.at[k], rs.at[k], place.along(k))
        c.start()
        direct.append(c)
    return direct, forwards


def forward_on(place, full, direct, forwards, xs, xr):
    for k in range(1, place.half):
        direct[k].wait_recv()
        got = full.at[place.hi_back(k) * 2 + place.lo]
        c = send(got, got, xs.at[k], xr.at[k], place.partner())
        c.start()
        forwards.append(c)


def gather_finish(place, full, direct, forwards, xs, xr):
    forward_on(place, full, direct, forwards, xs, xr)
    for k in range(1, place.half):
        direct[k].wait_send()
    for c in forwards:
        c.wait()


def scatter_start(place, part, rx, xs, xr):
    copies = [None] * place.half
    for k in list(range(1, place.half)) + [0]:
        c = send(part.at[place.hi_at(k) * 2 + 1 - place.lo], rx.at[k], xs.at[k], xr.at[k],
                 place.partner())
        c.start()
        copies[k] = c
    return copies


def scatter_middle(place, part, rx, stage, rz, copies, ss, rs):
    onward = [None]
    for k in range(1, place.half):
        copies[k].wait()
        total = part[place.hi_at(k) * 2 + place.lo].astype(F32) + rx[k].astype(F32)
        stage[k] = total.astype(BF16)
        c = send(stage.at[k], rz.at[k], ss.at[k], rs.at[k], place.along(k))
        c.start()
        onward.append(c)
    copies[0].wait()
    return onward


def scatter_finish(place, part, rx, rz, onward, out):
    total = part[place.hi * 2 + place.lo].astype(F32) + rx[0].astype(F32)
    for k in range(1, place.half):
        onward[k].wait()
        total = total + rz[k].astype(F32)
    out[...] = total


def norm_parts(values):
    average = jnp.mean(values, axis=-1, keepdims=True)
    centered = values - average
    variance = jnp.mean(centered * centered, axis=-1, keepdims=True)
    r = lax.rsqrt(variance + EPSILON)
    return centered * r, r


def norm_back(xhat, r, grad, gain):
    e = grad * gain
    return r * (
        e - jnp.mean(e, axis=-1, keepdims=True)
        - xhat * jnp.mean(e * xhat, axis=-1, keepdims=True)
    )


def column_sum(values):
    return jnp.sum(values, axis=0, keepdims=True)


def open_kernel(sizes, frames, weights, gain, shift, normed_g, w_full,
                mine, ns, nr, ws, wr, xs, xr):
    place = Place(sizes)
    greet(tensor_peers(place) + two_level_peers(place))
    direct, forwards = gather_start(place, weights, w_full, ws, wr, xs, xr)
    xhat, _ = norm_parts(frames[...].astype(F32))
    mine[...] = (xhat * gain[...] + shift[...]).astype(BF16)
    normeds = tensor_gather_start(place, mine, normed_g, ns, nr)
    normed_g[place.t] = mine[...]
    w_full[place.dp] = weights[...]
    gather_finish(place, w_full, direct, forwards, xs, xr)
    for c in normeds:
        c.wait()


GAPS = (1, -1, 2, -2, 3, -3)


def inside(place, g):
    return (place.dp + g >= 0) & (place.dp + g < place.n)


def greet_near(place, peers):
    barrier = pltpu.get_barrier_semaphore()
    for peer in peers:
        pl.semaphore_signal(barrier, inc=1, device_id=peer, device_id_type=MESH)
    for g in GAPS:
        @pl.when(inside(place, g))
        def _(g=g):
            pl.semaphore_signal(barrier, inc=1, device_id={"dp": place.dp + g},
                                device_id_type=MESH)
    pl.semaphore_wait(
        barrier, len(peers) + sum(inside(place, g).astype(jnp.int32) for g in GAPS)
    )


def dot(left, right, dims):
    return lax.dot_general(left, right, ((dims[:1], dims[1:]), ((), ())),
                           preferred_element_type=F32)


def attend_kernel(sizes, queries, kv, qid, kid, cot, weights,
                  attended, lse, window, cot_g, w_full,
                  ks, kr, cs, cr, ws, wr, xs, xr):
    place = Place(sizes)
    greet_near(place, tensor_peers(place) + two_level_peers(place))

    def copy(i, g):
        return send(kv, window.at[REACH - g], ks.at[i], kr.at[i], {"dp": place.dp + g})

    for i, g in enumerate(GAPS):
        @pl.when(inside(place, g))
        def _(i=i, g=g):
            copy(i, g).start()
    direct, forwards = gather_start(place, weights, w_full, ws, wr, xs, xr)
    cots = tensor_gather_start(place, cot, cot_g, cs, cr)
    window[REACH] = kv[...]
    cot_g[place.t] = cot[...]
    w_full[place.dp] = weights[...]
    for i, g in enumerate(GAPS):
        @pl.when(jnp.logical_not(inside(place, -g)))
        def _(g=g):
            window[REACH - g] = jnp.zeros_like(kv)
    for i, g in enumerate(GAPS):
        @pl.when(inside(place, g))
        def _(i=i, g=g):
            copy(i, g).wait_send()

        @pl.when(inside(place, -g))
        def _(i=i, g=g):
            copy(i, g).wait_recv()
    width = queries.shape[1]
    count = kid.shape[0]
    step = min(256, queries.shape[0])
    for h in range(width // HEAD):
        cols = slice(h * HEAD, (h + 1) * HEAD)
        vcols = slice(width + h * HEAD, width + (h + 1) * HEAD)
        for first in range(0, queries.shape[0], step):
            rows = slice(first, first + step)
            keys = window[:, :, cols].reshape(count, HEAD)
            values = window[:, :, vcols].reshape(count, HEAD)
            scores = dot(keys, queries[rows, cols], (1, 1)) * HEAD ** (-0.5)
            scores = jnp.where(kid[...] == qid[:, rows], scores, -1000000000.0)
            largest = jnp.max(scores, axis=0, keepdims=True)
            exps = jnp.exp(scores - largest)
            totals = jnp.sum(exps, axis=0, keepdims=True)
            probs = (exps * (1.0 / totals)).astype(BF16)
            lse[h:h + 1, rows] = largest + jnp.log(totals)
            attended[rows, cols] = dot(values, probs, (0, 0)).T.astype(BF16)
        if h == 0:
            forward_on(place, w_full, direct, forwards, xs, xr)
    for k in range(1, place.half):
        direct[k].wait_send()
    for c in forwards + cots:
        c.wait()


def middle_kernel(sizes, part, frames, gain, shift, bias, hidden, c_g,
                  slots, mine, ps, pr, cs, cr):
    place = Place(sizes)
    greet(tensor_peers(place))
    copies = tensor_scatter_start(place, part, slots, ps, pr)
    h = frames[...].astype(F32) + (tensor_scatter_sum(place, part, slots, copies) + bias[...])
    hidden[...] = h
    xhat, _ = norm_parts(h)
    mine[...] = (xhat * gain[...] + shift[...]).astype(BF16)
    sends = tensor_gather_start(place, mine, c_g, cs, cr)
    c_g[place.t] = mine[...]
    for c in sends:
        c.wait()


def turn_kernel(sizes, down, dc_part, hidden, cot, gain, bias, grads,
                encoded, dh_out, dz_g, vec, halves,
                slots_d, slots_c, mine, rx, ds, dr, cs, cr, zs, zr, xs, xr):
    place = Place(sizes)
    greet(tensor_peers(place) + [place.partner()])
    x_copies = scatter_start(place, grads, rx, xs, xr)
    c_copies = tensor_scatter_start(place, dc_part, slots_c, cs, cr)
    d_copies = tensor_scatter_start(place, down, slots_d, ds, dr)
    h = hidden[...]
    xhat, r = norm_parts(h)
    dc = tensor_scatter_sum(place, dc_part, slots_c, c_copies)
    dh = cot[...].astype(F32) + norm_back(xhat, r, dc, gain[...])
    dh_out[...] = dh
    dz = dh.astype(BF16)
    mine[...] = dz
    sends = tensor_gather_start(place, mine, dz_g, zs, zr)
    dz_g[place.t] = dz
    vec[0:1] = column_sum(dc * xhat)
    vec[1:2] = column_sum(dc)
    vec[2:3] = column_sum(dz.astype(F32))
    vec[3:4] = column_sum(cot[...].astype(F32))
    encoded[...] = (
        h + (tensor_scatter_sum(place, down, slots_d, d_copies) + bias[...])
    ).astype(BF16)
    for k in list(range(1, place.half)) + [0]:
        x_copies[k].wait()
        halves[k] = (
            grads[place.hi_at(k) * 2 + place.lo].astype(F32) + rx[k].astype(F32)
        ).astype(BF16)
    for c in sends:
        c.wait()


def back_kernel(sizes, queries, window, grad_out, lse, qid, kid, mlp, outs,
                dq, dkv_out, mlp_out, outs_out,
                probs, gprobs, dqt, dkv, slots, mz, rx, stage, rz,
                ks, kr, ms, mr, xs, xr, ss, rs):
    place = Place(sizes)
    greet_near(place, two_level_peers(place))
    copies = scatter_start(place, outs, rx, xs, xr)
    m_copies = [None]
    for k in range(1, place.half):
        c = send(mlp.at[k], mz.at[k], ms.at[k], mr.at[k], place.along(k))
        c.start()
        m_copies.append(c)

    def copy(i, g):
        return send(dkv.at[REACH + g], slots.at[i], ks.at[i], kr.at[i], {"dp": place.dp + g})

    width = queries.shape[1]
    heads = width // HEAD
    blocks, group = window.shape[0], window.shape[1]
    scale = HEAD ** (-0.5)
    order = [3, -3, 2, -2, 1, -1, 0]
    onward = None
    for h in range(heads):
        cols = slice(h * HEAD, (h + 1) * HEAD)
        vcols = slice(width + h * HEAD, width + (h + 1) * HEAD)

        def first(d, inner, h=h, cols=cols, vcols=vcols):
            scores = dot(window[d, :, cols], queries[:, cols], (1, 1)) * scale
            p = jnp.exp(jnp.where(kid[d] == qid[...], scores, -1000000000.0) - lse[h:h + 1])
            gp = dot(window[d, :, vcols], grad_out[:, cols], (1, 1))
            probs[d] = p
            gprobs[d] = gp
            return inner + jnp.sum(p * gp, axis=0, keepdims=True)

        inner = lax.fori_loop(0, blocks, first, jnp.zeros((1, group), F32))
        dqt[...] = jnp.zeros_like(dqt)

        def second(d, cols=cols, vcols=vcols, inner=inner):
            p = probs[d]
            ds = (p * (gprobs[d] - inner)).astype(BF16)
            dqt[...] += dot(window[d, :, cols], ds, (0, 0))
            dkv[d, :, cols] = (dot(ds, queries[:, cols], (1, 0)) * scale).astype(BF16)
            dkv[d, :, vcols] = dot(p.astype(BF16), grad_out[:, cols], (1, 0)).astype(BF16)

        if h < heads - 1:
            def step(d, carry, second=second):
                second(d)
                return carry

            lax.fori_loop(0, blocks, step, 0)
        else:
            for g in order:
                second(REACH + g)
                if g:
                    @pl.when(inside(place, g))
                    def _(g=g):
                        copy(GAPS.index(g), g).start()
        dq[:, cols] = (dqt[...].T * scale).astype(BF16)
        if h == 0:
            onward = scatter_middle(place, outs, rx, stage, rz, copies, ss, rs)
    dkv_out[...] = dkv[REACH].astype(F32)
    scatter_finish(place, outs, rx, rz, onward, outs_out)
    total = mlp[0].astype(F32)
    for k in range(1, place.half):
        m_copies[k].wait()
        total = total + mz[k].astype(F32)
    mlp_out[...] = total
    for g in order[:-1]:
        i = GAPS.index(g)

        @pl.when(inside(place, g))
        def _(i=i, g=g):
            copy(i, g).wait_send()

        @pl.when(inside(place, -g))
        def _(i=i, g=g):
            copy(i, g).wait_recv()
            dkv_out[...] += slots[i].astype(F32)


def close_kernel(sizes, da_part, frames, dh, gain, grads, vec_in, frames_grad, grads_out, vec_out,
                 slots, rx, stage, rz, vec, vt, vsum, vx, vpair, vz,
                 ps, pr, xs, xr, ss, rs, vs, vr, us, ur, zs, zr):
    place = Place(sizes)
    greet(tensor_peers(place) + two_level_peers(place))
    copies = tensor_scatter_start(place, da_part, slots, ps, pr)
    x_copies = scatter_start(place, grads, rx, xs, xr)
    xhat, r = norm_parts(frames[...].astype(F32))
    da = tensor_scatter_sum(place, da_part, slots, copies)
    frames_grad[...] = (dh[...] + norm_back(xhat, r, da, gain[...])).astype(BF16)
    vec[...] = vec_in[...]
    vec[0:1] = column_sum(da * xhat)
    vec[2:3] = column_sum(da)
    v_copies = []
    for k in range(1, place.t_count):
        c = send(vec, vt.at[k - 1], vs.at[k], vr.at[k], {"tensor": place.tensor_at(k)})
        c.start()
        v_copies.append(c)
    onward = scatter_middle(place, grads, rx, stage, rz, x_copies, ss, rs)
    for c in v_copies:
        c.wait()
    vsum[place.t] = vec[...]
    for k in range(1, place.t_count):
        vsum[place.tensor_back(k)] = vt[k - 1]
    total = vsum[0]
    for k in range(1, place.t_count):
        total = total + vsum[k]
    vx[0] = total
    c = send(vx.at[0], vx.at[1], us.at[0], ur.at[0], place.partner())
    c.start()
    c.wait()
    vpair[...] = vx[0] + vx[1]
    vz[place.hi] = vpair[...]
    z_copies = []
    for k in range(1, place.half):
        c = send(vpair, vz.at[place.hi], zs.at[k], zr.at[k], place.along(k))
        c.start()
        z_copies.append(c)
    scatter_finish(place, grads, rx, rz, onward, grads_out)
    for c in z_copies:
        c.wait()
    total = vz[0]
    for k in range(1, place.half):
        total = total + vz[k]
    vec_out[...] = total


def call(kernel, sizes, ident, outs, scratch, *args):
    return pl.pallas_call(
        partial(kernel, sizes),
        out_shape=[jax.ShapeDtypeStruct(s, t) for s, t in outs],
        in_specs=[VMEM] * len(args),
        out_specs=[VMEM] * len(outs),
        scratch_shapes=scratch,
        compiler_params=pltpu.CompilerParams(
            collective_id=ident, has_side_effects=True, vmem_limit_bytes=LIMIT
        ),
    )(*args)


def clip_ids(positions, clip_offsets):
    return jnp.sum((positions[:, None] >= clip_offsets[None, :]).astype(jnp.int32), axis=1) - 1


def contract_rows(left, right):
    return lax.dot_general(
        left, right, (((0,), (0,)), ((), ())), preferred_element_type=jnp.float32
    )


def contract_cols(left, right):
    return lax.dot_general(
        left, right, (((1,), (1,)), ((), ())), preferred_element_type=jnp.float32
    )


def place_slice(piece, tensor_idx, full_width):
    return lax.dynamic_update_slice_in_dim(
        jnp.zeros((full_width,), F32), piece, tensor_idx * piece.shape[0], 0
    )


def shards(
    frames, clip_offsets, qkv_weight, out_weight, up_weight, down_weight,
    ln_gain, ln_bias, proj_bias, fc_bias, out_cotangent,
):
    t_idx = lax.axis_index("tensor")
    dp_idx = lax.axis_index("dp")
    n = lax.axis_size("dp")
    t_count = lax.axis_size("tensor")
    sizes = (n, t_count)
    half = n // 2
    rows = frames.shape[0]
    group = rows * t_count
    wrows = qkv_weight.shape[1]
    width = qkv_weight.shape[3]
    ff = up_weight.shape[2]
    ff_all = fc_bias.shape[1]
    gains, shifts, pbias, fbias = ln_gain[0], ln_bias[0], proj_bias[0], fc_bias[0]

    w_local = jnp.concatenate([out_weight[0].T, up_weight[0], down_weight[0].T], axis=1)
    w_qkv = qkv_weight[0].reshape(wrows, 3 * width)
    total = w_local.shape[1]
    t3 = (t_count, rows, D)
    normed_g, qkv_full = call(
        open_kernel, sizes, 1,
        [(t3, BF16), ((n, wrows, 3 * width), BF16)],
        [pltpu.VMEM((rows, D), BF16), dma(t_count), dma(t_count),
         dma(half), dma(half), dma(half), dma(half)],
        frames, w_qkv, gains[0:1], shifts[0:1],
    )
    normed_g = normed_g.reshape(group, D)
    qkv_full = qkv_full.reshape(D, 3 * width)

    q_bias = lax.dynamic_slice_in_dim(pbias[0], t_idx * width, width)
    v_bias = lax.dynamic_slice_in_dim(pbias[1], t_idx * width, width)
    bias_row = jnp.concatenate([q_bias, jnp.zeros_like(q_bias), v_bias])
    projected = (jnp.dot(normed_g, qkv_full, preferred_element_type=F32) + bias_row).astype(BF16)
    queries = projected[:, :width]
    blocks = 2 * REACH + 1
    query_pos = dp_idx * group + jnp.arange(group, dtype=jnp.int32)
    key_pos = (dp_idx - REACH) * group + jnp.arange(blocks * group, dtype=jnp.int32)
    qid = clip_ids(query_pos, clip_offsets)[None]
    kid = jnp.where(
        (key_pos >= 0) & (key_pos < n * group), clip_ids(key_pos, clip_offsets), -2
    )[:, None]
    heads = width // HEAD
    attended, lse, window, cot_g, w_full = call(
        attend_kernel, sizes, 2,
        [((group, width), BF16), ((heads, group), F32), ((blocks, group, 2 * width), BF16),
         (t3, BF16), ((n, wrows, total), BF16)],
        [dma(6), dma(6), dma(t_count), dma(t_count), dma(half), dma(half), dma(half), dma(half)],
        queries, projected[:, width:], qid, kid, out_cotangent, w_local,
    )
    cot_g = cot_g.reshape(group, D)
    w_full = w_full.reshape(D, total)
    out_t = w_full[:, :width]
    up_full = w_full[:, width:width + ff]
    down_t = w_full[:, width + ff:]

    part = contract_cols(attended, out_t).astype(BF16).reshape(t3)
    hidden, c_g = call(
        middle_kernel, sizes, 3, [((rows, D), F32), (t3, BF16)],
        [pltpu.VMEM((t_count - 1, rows, D), BF16), pltpu.VMEM((rows, D), BF16)]
        + [dma(t_count)] * 4,
        part, frames, gains[1:2], shifts[1:2], pbias[2:3],
    )
    c_g = c_g.reshape(group, D)
    upper = jnp.dot(c_g, up_full, preferred_element_type=F32)
    upper = upper + lax.dynamic_slice_in_dim(fbias, t_idx * ff, ff)
    cdf = 0.5 * (1.0 + lax.erf(upper * (2.0 ** -0.5)))
    activated = (upper * cdf).astype(BF16)
    down_part = contract_cols(activated, down_t).astype(BF16).reshape(t3)

    slope = cdf + upper * jnp.exp(-0.5 * upper * upper) * 0.3989422804014327
    grad_act = jnp.dot(cot_g, down_t, preferred_element_type=F32)
    grad_upper = (grad_act * slope).astype(BF16)
    dc_part = contract_cols(grad_upper, up_full).astype(BF16).reshape(t3)
    down_grad_t = contract_rows(cot_g, activated)
    up_grad = contract_rows(c_g, grad_upper)
    mlp = jnp.concatenate([up_grad, down_grad_t], axis=1).astype(BF16).reshape(n, wrows, 2 * ff)
    mlp_blocks = pltpu.VMEM((half, wrows, 2 * ff), BF16)
    encoded, dh, dz_g, vec2, mlp = call(
        turn_kernel, sizes, 4,
        [((rows, D), BF16), ((rows, D), F32), (t3, BF16), ((4, D), F32),
         ((half, wrows, 2 * ff), BF16)],
        [pltpu.VMEM((t_count - 1, rows, D), BF16), pltpu.VMEM((t_count - 1, rows, D), BF16),
         pltpu.VMEM((rows, D), BF16), mlp_blocks] + [dma(t_count)] * 6 + [dma(half)] * 2,
        down_part, dc_part, hidden, out_cotangent, gains[1:2], pbias[3:4], mlp,
    )
    dz_g = dz_g.reshape(group, D)
    fc_grad = place_slice(jnp.sum(grad_upper, axis=0, dtype=F32), t_idx, ff_all)
    outs = contract_rows(dz_g, attended).astype(BF16).reshape(n, wrows, width)
    grad_attended = jnp.dot(dz_g, out_t, preferred_element_type=F32).astype(BF16)
    grad_queries, dkv_sum, mlp, out_grad = call(
        back_kernel, sizes, 5,
        [((group, width), BF16), ((group, 2 * width), F32), ((wrows, 2 * ff), F32),
         ((wrows, width), F32)],
        [pltpu.VMEM((blocks, group, group), F32)] * 2 + [pltpu.VMEM((HEAD, group), F32)]
        + [pltpu.VMEM((blocks, group, 2 * width), BF16), pltpu.VMEM((6, group, 2 * width), BF16)]
        + [mlp_blocks] + [pltpu.VMEM((half, wrows, width), BF16)] * 3
        + [dma(6)] * 2 + [dma(half)] * 6,
        queries, window, grad_attended, lse, qid, kid.reshape(blocks, group, 1), mlp, outs,
    )
    out_grad = out_grad.T
    up_grad = mlp[:, :ff]
    down_grad = mlp[:, ff:].T

    grad_proj = jnp.concatenate([grad_queries, dkv_sum.astype(BF16)], axis=1)
    qkv_grad = contract_rows(normed_g, grad_proj).astype(BF16)
    bias_sums = jnp.sum(grad_proj, axis=0, dtype=F32)
    da_part = contract_cols(grad_proj, qkv_full).astype(BF16).reshape(t3)
    zero = jnp.zeros((1, D), F32)
    vec = jnp.concatenate([
        zero, vec2[0:1], zero, vec2[1:2],
        place_slice(bias_sums[:width], t_idx, D)[None],
        place_slice(bias_sums[2 * width:], t_idx, D)[None],
        vec2[2:4], fc_grad.reshape(-1, D), zero, zero, zero, zero,
    ], axis=0)
    vshape = vec.shape
    frames_grad, qkv_grad, vec = call(
        close_kernel, sizes, 6,
        [((rows, D), BF16), ((wrows, 3 * width), F32), (vshape, F32)],
        [pltpu.VMEM((t_count - 1, rows, D), BF16)]
        + [pltpu.VMEM((half, wrows, 3 * width), BF16)] * 3
        + [pltpu.VMEM(vshape, F32), pltpu.VMEM((t_count - 1,) + vshape, F32),
           pltpu.VMEM((t_count,) + vshape, F32), pltpu.VMEM((2,) + vshape, F32),
           pltpu.VMEM(vshape, F32), pltpu.VMEM((half,) + vshape, F32)]
        + [dma(t_count)] * 2 + [dma(half)] * 4 + [dma(t_count)] * 2 + [dma(1)] * 2
        + [dma(half)] * 2,
        da_part, frames, dh, gains[0:1], qkv_grad.reshape(n, wrows, 3 * width), vec,
    )
    fc_rows = ff_all // D
    return (
        encoded,
        frames_grad,
        qkv_grad.reshape(1, wrows, 3, width),
        out_grad[None],
        up_grad[None],
        down_grad[None],
        vec[None, 0:2],
        vec[None, 2:4],
        vec[None, 4:8],
        vec[8:8 + fc_rows].reshape(1, ff_all),
    )


def solution(mesh):
    return jax.shard_map(
        shards,
        mesh=mesh,
        in_specs=(
            P(("dp", "tensor"), None),
            P(),
            P(None, "dp", None, "tensor"),
            P(None, "tensor", "dp"),
            P(None, "dp", "tensor"),
            P(None, "tensor", "dp"),
            P(),
            P(),
            P(),
            P(),
            P(("dp", "tensor"), None),
        ),
        out_specs=(
            P(("dp", "tensor"), None),
            P(("dp", "tensor"), None),
            P(None, "dp", None, "tensor"),
            P(None, "tensor", "dp"),
            P(None, "dp", "tensor"),
            P(None, "tensor", "dp"),
            P(),
            P(),
            P(),
            P(),
        ),
        check_vma=False,
    )
```

```python
from functools import partial

import jax
import jax.numpy as jnp
from jax import lax
from jax.experimental import pallas as pl
from jax.experimental.pallas import tpu as pltpu
from jax.sharding import PartitionSpec as P

D = 768
HEAD = 64
REACH = 3
EPSILON = 1e-05
MESH = pl.DeviceIdType.MESH
F32 = jnp.float32
BF16 = jnp.bfloat16
VMEM = pl.BlockSpec(memory_space=pltpu.VMEM)
LIMIT = 56 * 1024 * 1024


def dma(n):
    return pltpu.SemaphoreType.DMA((n,))


def send(src, dst, send_sem, recv_sem, where):
    return pltpu.make_async_remote_copy(
        src_ref=src, dst_ref=dst, send_sem=send_sem, recv_sem=recv_sem,
        device_id=where, device_id_type=MESH,
    )


class Place:
    def __init__(self, sizes):
        self.n, self.t_count = sizes
        self.half = self.n // 2
        self.dp = lax.axis_index("dp")
        self.t = lax.axis_index("tensor")
        self.hi = lax.div(self.dp, 2)
        self.lo = lax.rem(self.dp, 2)

    def tensor_at(self, k):
        return lax.rem(self.t + k, self.t_count)

    def tensor_back(self, k):
        return lax.rem(self.t + self.t_count - k, self.t_count)

    def hi_at(self, k):
        return lax.rem(self.hi + k, self.half)

    def hi_back(self, k):
        return lax.rem(self.hi + self.half - k, self.half)

    def partner(self):
        return {"dp": self.hi * 2 + 1 - self.lo}

    def along(self, k):
        return {"dp": self.hi_at(k) * 2 + self.lo}


def greet(peers):
    barrier = pltpu.get_barrier_semaphore()
    for peer in peers:
        pl.semaphore_signal(barrier, inc=1, device_id=peer, device_id_type=MESH)
    pl.semaphore_wait(barrier, len(peers))


def tensor_peers(place):
    return [{"tensor": place.tensor_at(k)} for k in range(1, place.t_count)]


def two_level_peers(place):
    return [place.partner()] + [place.along(k) for k in range(1, place.half)]


def tensor_gather_start(place, src, group, ss, rs):
    copies = []
    for k in range(1, place.t_count):
        c = send(src, group.at[place.t], ss.at[k], rs.at[k], {"tensor": place.tensor_at(k)})
        c.start()
        copies.append(c)
    return copies


def tensor_scatter_start(place, part, slots, ss, rs):
    copies = []
    for k in range(1, place.t_count):
        c = send(part.at[place.tensor_at(k)], slots.at[k - 1], ss.at[k], rs.at[k],
                 {"tensor": place.tensor_at(k)})
        c.start()
        copies.append(c)
    return copies


def tensor_scatter_sum(place, part, slots, copies):
    total = part[place.t].astype(F32)
    for k in range(1, place.t_count):
        copies[k - 1].wait()
        total = total + slots[k - 1].astype(F32)
    return total


def gather_start(place, local, full, ss, rs, xs, xr):
    direct = [None]
    forwards = []
    mine = place.dp
    c = send(local, full.at[mine], xs.at[0], xr.at[0], place.partner())
    c.start()
    forwards.append(c)
    for k in range(1, place.half):
        c = send(local, full.at[mine], ss.at[k], rs.at[k], place.along(k))
        c.start()
        direct.append(c)
    return direct, forwards


def forward_on(place, full, direct, forwards, xs, xr):
    for k in range(1, place.half):
        direct[k].wait_recv()
        got = full.at[place.hi_back(k) * 2 + place.lo]
        c = send(got, got, xs.at[k], xr.at[k], place.partner())
        c.start()
        forwards.append(c)


def gather_finish(place, full, direct, forwards, xs, xr):
    forward_on(place, full, direct, forwards, xs, xr)
    for k in range(1, place.half):
        direct[k].wait_send()
    for c in forwards:
        c.wait()


def scatter_start(place, part, rx, xs, xr):
    copies = [None] * place.half
    for k in list(range(1, place.half)) + [0]:
        c = send(part.at[place.hi_at(k) * 2 + 1 - place.lo], rx.at[k], xs.at[k], xr.at[k],
                 place.partner())
        c.start()
        copies[k] = c
    return copies


def scatter_middle(place, part, rx, stage, rz, copies, ss, rs):
    onward = [None]
    for k in range(1, place.half):
        copies[k].wait()
        total = part[place.hi_at(k) * 2 + place.lo].astype(F32) + rx[k].astype(F32)
        stage[k] = total.astype(BF16)
        c = send(stage.at[k], rz.at[k], ss.at[k], rs.at[k], place.along(k))
        c.start()
        onward.append(c)
    copies[0].wait()
    return onward


def scatter_finish(place, part, rx, rz, onward, out):
    total = part[place.hi * 2 + place.lo].astype(F32) + rx[0].astype(F32)
    for k in range(1, place.half):
        onward[k].wait()
        total = total + rz[k].astype(F32)
    out[...] = total


def norm_parts(values):
    average = jnp.mean(values, axis=-1, keepdims=True)
    centered = values - average
    variance = jnp.mean(centered * centered, axis=-1, keepdims=True)
    r = lax.rsqrt(variance + EPSILON)
    return centered * r, r


def norm_back(xhat, r, grad, gain):
    e = grad * gain
    return r * (
        e - jnp.mean(e, axis=-1, keepdims=True)
        - xhat * jnp.mean(e * xhat, axis=-1, keepdims=True)
    )


def column_sum(values):
    return jnp.sum(values, axis=0, keepdims=True)


def open_kernel(sizes, frames, weights, gain, shift, normed_g, w_full,
                mine, ns, nr, ws, wr, xs, xr):
    place = Place(sizes)
    greet(tensor_peers(place) + two_level_peers(place))
    direct, forwards = gather_start(place, weights, w_full, ws, wr, xs, xr)
    xhat, _ = norm_parts(frames[...].astype(F32))
    mine[...] = (xhat * gain[...] + shift[...]).astype(BF16)
    normeds = tensor_gather_start(place, mine, normed_g, ns, nr)
    normed_g[place.t] = mine[...]
    w_full[place.dp] = weights[...]
    gather_finish(place, w_full, direct, forwards, xs, xr)
    for c in normeds:
        c.wait()


GAPS = (1, -1, 2, -2, 3, -3)


def inside(place, g):
    return (place.dp + g >= 0) & (place.dp + g < place.n)


def greet_near(place, peers):
    barrier = pltpu.get_barrier_semaphore()
    for peer in peers:
        pl.semaphore_signal(barrier, inc=1, device_id=peer, device_id_type=MESH)
    for g in GAPS:
        @pl.when(inside(place, g))
        def _(g=g):
            pl.semaphore_signal(barrier, inc=1, device_id={"dp": place.dp + g},
                                device_id_type=MESH)
    pl.semaphore_wait(
        barrier, len(peers) + sum(inside(place, g).astype(jnp.int32) for g in GAPS)
    )


def dot(left, right, dims):
    return lax.dot_general(left, right, ((dims[:1], dims[1:]), ((), ())),
                           preferred_element_type=F32)


def attend_kernel(sizes, queries, kv, qid, kid, cot, weights, mlp,
                  attended, lse, window, cot_g, w_full, have, mate,
                  ks, kr, cs, cr, ws, wr, xs, xr, ms, mr):
    place = Place(sizes)
    greet_near(place, tensor_peers(place) + two_level_peers(place))

    def copy(i, g):
        return send(kv, window.at[REACH - g], ks.at[i], kr.at[i], {"dp": place.dp + g})

    for i, g in enumerate(GAPS):
        @pl.when(inside(place, g))
        def _(i=i, g=g):
            copy(i, g).start()
    direct, forwards = gather_start(place, weights, w_full, ws, wr, xs, xr)
    cots = tensor_gather_start(place, cot, cot_g, cs, cr)
    window[REACH] = kv[...]
    cot_g[place.t] = cot[...]
    w_full[place.dp] = weights[...]
    for i, g in enumerate(GAPS):
        @pl.when(jnp.logical_not(inside(place, -g)))
        def _(g=g):
            window[REACH - g] = jnp.zeros_like(kv)
    for i, g in enumerate(GAPS):
        @pl.when(inside(place, g))
        def _(i=i, g=g):
            copy(i, g).wait_send()

        @pl.when(inside(place, -g))
        def _(i=i, g=g):
            copy(i, g).wait_recv()
    m_copies = []
    for k in range(1, place.half):
        m_copies.append(send(mlp, have.at[k], ms.at[k], mr.at[k], place.along(k)))
    m_copies.append(send(mlp, mate, ms.at[0], mr.at[0], place.partner()))
    for c in m_copies:
        c.start()
    have[0] = mlp[...]
    width = queries.shape[1]
    count = kid.shape[0]
    step = min(256, queries.shape[0])
    for h in range(width // HEAD):
        cols = slice(h * HEAD, (h + 1) * HEAD)
        vcols = slice(width + h * HEAD, width + (h + 1) * HEAD)
        for first in range(0, queries.shape[0], step):
            rows = slice(first, first + step)
            keys = window[:, :, cols].reshape(count, HEAD)
            values = window[:, :, vcols].reshape(count, HEAD)
            scores = dot(keys, queries[rows, cols], (1, 1)) * HEAD ** (-0.5)
            scores = jnp.where(kid[...] == qid[:, rows], scores, -1000000000.0)
            largest = jnp.max(scores, axis=0, keepdims=True)
            exps = jnp.exp(scores - largest)
            totals = jnp.sum(exps, axis=0, keepdims=True)
            probs = (exps * (1.0 / totals)).astype(BF16)
            lse[h:h + 1, rows] = largest + jnp.log(totals)
            attended[rows, cols] = dot(values, probs, (0, 0)).T.astype(BF16)
        if h == 0:
            forward_on(place, w_full, direct, forwards, xs, xr)
    for k in range(1, place.half):
        direct[k].wait_send()
    for c in forwards + cots + m_copies:
        c.wait()


def middle_kernel(sizes, part, frames, gain, shift, bias, have, mate, hidden, c_g, mlp_full,
                  slots, mine, ps, pr, cs, cr, xs, xr):
    place = Place(sizes)
    greet(tensor_peers(place) + [place.partner()])
    copies = tensor_scatter_start(place, part, slots, ps, pr)
    forwards = []
    for k in range(1, place.half):
        c = send(have.at[k], mlp_full.at[place.hi_back(k) * 2 + place.lo], xs.at[k], xr.at[k],
                 place.partner())
        c.start()
        forwards.append(c)
    for k in range(place.half):
        mlp_full[place.hi_back(k) * 2 + place.lo] = have[k]
    mlp_full[place.hi * 2 + 1 - place.lo] = mate[...]
    h = frames[...].astype(F32) + (tensor_scatter_sum(place, part, slots, copies) + bias[...])
    hidden[...] = h
    xhat, _ = norm_parts(h)
    mine[...] = (xhat * gain[...] + shift[...]).astype(BF16)
    sends = tensor_gather_start(place, mine, c_g, cs, cr)
    c_g[place.t] = mine[...]
    for c in sends + forwards:
        c.wait()


def turn_kernel(sizes, down, dc_part, hidden, cot, gain, bias, grads,
                encoded, dh_out, dz_g, vec, halves,
                slots_d, slots_c, mine, rx, ds, dr, cs, cr, zs, zr, xs, xr):
    place = Place(sizes)
    greet(tensor_peers(place) + [place.partner()])
    x_copies = scatter_start(place, grads, rx, xs, xr)
    c_copies = tensor_scatter_start(place, dc_part, slots_c, cs, cr)
    d_copies = tensor_scatter_start(place, down, slots_d, ds, dr)
    h = hidden[...]
    xhat, r = norm_parts(h)
    dc = tensor_scatter_sum(place, dc_part, slots_c, c_copies)
    dh = cot[...].astype(F32) + norm_back(xhat, r, dc, gain[...])
    dh_out[...] = dh
    dz = dh.astype(BF16)
    mine[...] = dz
    sends = tensor_gather_start(place, mine, dz_g, zs, zr)
    dz_g[place.t] = dz
    vec[0:1] = column_sum(dc * xhat)
    vec[1:2] = column_sum(dc)
    vec[2:3] = column_sum(dz.astype(F32))
    vec[3:4] = column_sum(cot[...].astype(F32))
    encoded[...] = (
        h + (tensor_scatter_sum(place, down, slots_d, d_copies) + bias[...])
    ).astype(BF16)
    for k in list(range(1, place.half)) + [0]:
        x_copies[k].wait()
        halves[k] = (
            grads[place.hi_at(k) * 2 + place.lo].astype(F32) + rx[k].astype(F32)
        ).astype(BF16)
    for c in sends:
        c.wait()


def back_kernel(sizes, queries, window, grad_out, lse, qid, kid, mlp, outs,
                dq, dkv_out, mlp_out, outs_out,
                probs, gprobs, dqt, dkv, slots, mz, rx, stage, rz,
                ks, kr, ms, mr, xs, xr, ss, rs):
    place = Place(sizes)
    greet_near(place, two_level_peers(place))
    copies = scatter_start(place, outs, rx, xs, xr)
    m_copies = [None]
    for k in range(1, place.half):
        c = send(mlp.at[k], mz.at[k], ms.at[k], mr.at[k], place.along(k))
        c.start()
        m_copies.append(c)

    def copy(i, g):
        return send(dkv.at[REACH + g], slots.at[i], ks.at[i], kr.at[i], {"dp": place.dp + g})

    width = queries.shape[1]
    heads = width // HEAD
    blocks, group = window.shape[0], window.shape[1]
    scale = HEAD ** (-0.5)
    order = [3, -3, 2, -2, 1, -1, 0]
    onward = None
    for h in range(heads):
        cols = slice(h * HEAD, (h + 1) * HEAD)
        vcols = slice(width + h * HEAD, width + (h + 1) * HEAD)

        def first(d, inner, h=h, cols=cols, vcols=vcols):
            scores = dot(window[d, :, cols], queries[:, cols], (1, 1)) * scale
            p = jnp.exp(jnp.where(kid[d] == qid[...], scores, -1000000000.0) - lse[h:h + 1])
            gp = dot(window[d, :, vcols], grad_out[:, cols], (1, 1))
            probs[d] = p
            gprobs[d] = gp
            return inner + jnp.sum(p * gp, axis=0, keepdims=True)

        inner = lax.fori_loop(0, blocks, first, jnp.zeros((1, group), F32))
        dqt[...] = jnp.zeros_like(dqt)

        def second(d, cols=cols, vcols=vcols, inner=inner):
            p = probs[d]
            ds = (p * (gprobs[d] - inner)).astype(BF16)
            dqt[...] += dot(window[d, :, cols], ds, (0, 0))
            dkv[d, :, cols] = (dot(ds, queries[:, cols], (1, 0)) * scale).astype(BF16)
            dkv[d, :, vcols] = dot(p.astype(BF16), grad_out[:, cols], (1, 0)).astype(BF16)

        if h < heads - 1:
            def step(d, carry, second=second):
                second(d)
                return carry

            lax.fori_loop(0, blocks, step, 0)
        else:
            for g in order:
                second(REACH + g)
                if g:
                    @pl.when(inside(place, g))
                    def _(g=g):
                        copy(GAPS.index(g), g).start()
        dq[:, cols] = (dqt[...].T * scale).astype(BF16)
        if h == 0:
            onward = scatter_middle(place, outs, rx, stage, rz, copies, ss, rs)
    dkv_out[...] = dkv[REACH].astype(F32)
    scatter_finish(place, outs, rx, rz, onward, outs_out)
    total = mlp[0].astype(F32)
    for k in range(1, place.half):
        m_copies[k].wait()
        total = total + mz[k].astype(F32)
    mlp_out[...] = total
    for g in order[:-1]:
        i = GAPS.index(g)

        @pl.when(inside(place, g))
        def _(i=i, g=g):
            copy(i, g).wait_send()

        @pl.when(inside(place, -g))
        def _(i=i, g=g):
            copy(i, g).wait_recv()
            dkv_out[...] += slots[i].astype(F32)


def close_kernel(sizes, da_part, frames, dh, gain, grads, vec_in, frames_grad, grads_out, vec_out,
                 slots, rx, stage, rz, vec, vt, vsum, vx, vpair, vz,
                 ps, pr, xs, xr, ss, rs, vs, vr, us, ur, zs, zr):
    place = Place(sizes)
    greet(tensor_peers(place) + two_level_peers(place))
    copies = tensor_scatter_start(place, da_part, slots, ps, pr)
    x_copies = scatter_start(place, grads, rx, xs, xr)
    xhat, r = norm_parts(frames[...].astype(F32))
    da = tensor_scatter_sum(place, da_part, slots, copies)
    frames_grad[...] = (dh[...] + norm_back(xhat, r, da, gain[...])).astype(BF16)
    vec[...] = vec_in[...]
    vec[0:1] = column_sum(da * xhat)
    vec[2:3] = column_sum(da)
    v_copies = []
    for k in range(1, place.t_count):
        c = send(vec, vt.at[k - 1], vs.at[k], vr.at[k], {"tensor": place.tensor_at(k)})
        c.start()
        v_copies.append(c)
    onward = scatter_middle(place, grads, rx, stage, rz, x_copies, ss, rs)
    for c in v_copies:
        c.wait()
    vsum[place.t] = vec[...]
    for k in range(1, place.t_count):
        vsum[place.tensor_back(k)] = vt[k - 1]
    total = vsum[0]
    for k in range(1, place.t_count):
        total = total + vsum[k]
    vx[0] = total
    c = send(vx.at[0], vx.at[1], us.at[0], ur.at[0], place.partner())
    c.start()
    c.wait()
    vpair[...] = vx[0] + vx[1]
    vz[place.hi] = vpair[...]
    z_copies = []
    for k in range(1, place.half):
        c = send(vpair, vz.at[place.hi], zs.at[k], zr.at[k], place.along(k))
        c.start()
        z_copies.append(c)
    scatter_finish(place, grads, rx, rz, onward, grads_out)
    for c in z_copies:
        c.wait()
    total = vz[0]
    for k in range(1, place.half):
        total = total + vz[k]
    vec_out[...] = total


def call(kernel, sizes, ident, outs, scratch, *args):
    return pl.pallas_call(
        partial(kernel, sizes),
        out_shape=[jax.ShapeDtypeStruct(s, t) for s, t in outs],
        in_specs=[VMEM] * len(args),
        out_specs=[VMEM] * len(outs),
        scratch_shapes=scratch,
        compiler_params=pltpu.CompilerParams(
            collective_id=ident, has_side_effects=True, vmem_limit_bytes=LIMIT
        ),
    )(*args)


def clip_ids(positions, clip_offsets):
    return jnp.sum((positions[:, None] >= clip_offsets[None, :]).astype(jnp.int32), axis=1) - 1


def contract_rows(left, right):
    return lax.dot_general(
        left, right, (((0,), (0,)), ((), ())), preferred_element_type=jnp.float32
    )


def contract_cols(left, right):
    return lax.dot_general(
        left, right, (((1,), (1,)), ((), ())), preferred_element_type=jnp.float32
    )


def place_slice(piece, tensor_idx, full_width):
    return lax.dynamic_update_slice_in_dim(
        jnp.zeros((full_width,), F32), piece, tensor_idx * piece.shape[0], 0
    )


def shards(
    frames, clip_offsets, qkv_weight, out_weight, up_weight, down_weight,
    ln_gain, ln_bias, proj_bias, fc_bias, out_cotangent,
):
    t_idx = lax.axis_index("tensor")
    dp_idx = lax.axis_index("dp")
    n = lax.axis_size("dp")
    t_count = lax.axis_size("tensor")
    sizes = (n, t_count)
    half = n // 2
    rows = frames.shape[0]
    group = rows * t_count
    wrows = qkv_weight.shape[1]
    width = qkv_weight.shape[3]
    ff = up_weight.shape[2]
    ff_all = fc_bias.shape[1]
    gains, shifts, pbias, fbias = ln_gain[0], ln_bias[0], proj_bias[0], fc_bias[0]

    w_mlp = jnp.concatenate([up_weight[0], down_weight[0].T], axis=1)
    w_qkv = qkv_weight[0].reshape(wrows, 3 * width)
    t3 = (t_count, rows, D)
    normed_g, qkv_full = call(
        open_kernel, sizes, 1,
        [(t3, BF16), ((n, wrows, 3 * width), BF16)],
        [pltpu.VMEM((rows, D), BF16), dma(t_count), dma(t_count),
         dma(half), dma(half), dma(half), dma(half)],
        frames, w_qkv, gains[0:1], shifts[0:1],
    )
    normed_g = normed_g.reshape(group, D)
    qkv_full = qkv_full.reshape(D, 3 * width)

    q_bias = lax.dynamic_slice_in_dim(pbias[0], t_idx * width, width)
    v_bias = lax.dynamic_slice_in_dim(pbias[1], t_idx * width, width)
    bias_row = jnp.concatenate([q_bias, jnp.zeros_like(q_bias), v_bias])
    projected = (jnp.dot(normed_g, qkv_full, preferred_element_type=F32) + bias_row).astype(BF16)
    queries = projected[:, :width]
    blocks = 2 * REACH + 1
    query_pos = dp_idx * group + jnp.arange(group, dtype=jnp.int32)
    key_pos = (dp_idx - REACH) * group + jnp.arange(blocks * group, dtype=jnp.int32)
    qid = clip_ids(query_pos, clip_offsets)[None]
    kid = jnp.where(
        (key_pos >= 0) & (key_pos < n * group), clip_ids(key_pos, clip_offsets), -2
    )[:, None]
    heads = width // HEAD
    attended, lse, window, cot_g, out_t, have, mate = call(
        attend_kernel, sizes, 2,
        [((group, width), BF16), ((heads, group), F32), ((blocks, group, 2 * width), BF16),
         (t3, BF16), ((n, wrows, width), BF16), ((half, wrows, 2 * ff), BF16),
         ((wrows, 2 * ff), BF16)],
        [dma(6), dma(6), dma(t_count), dma(t_count)] + [dma(half)] * 6,
        queries, projected[:, width:], qid, kid, out_cotangent, out_weight[0].T, w_mlp,
    )
    cot_g = cot_g.reshape(group, D)
    out_t = out_t.reshape(D, width)

    part = contract_cols(attended, out_t).astype(BF16).reshape(t3)
    hidden, c_g, mlp_full = call(
        middle_kernel, sizes, 3, [((rows, D), F32), (t3, BF16), ((n, wrows, 2 * ff), BF16)],
        [pltpu.VMEM((t_count - 1, rows, D), BF16), pltpu.VMEM((rows, D), BF16)]
        + [dma(t_count)] * 4 + [dma(half)] * 2,
        part, frames, gains[1:2], shifts[1:2], pbias[2:3], have, mate,
    )
    mlp_full = mlp_full.reshape(D, 2 * ff)
    up_full, down_t = mlp_full[:, :ff], mlp_full[:, ff:]
    c_g = c_g.reshape(group, D)
    upper = jnp.dot(c_g, up_full, preferred_element_type=F32)
    upper = upper + lax.dynamic_slice_in_dim(fbias, t_idx * ff, ff)
    cdf = 0.5 * (1.0 + lax.erf(upper * (2.0 ** -0.5)))
    activated = (upper * cdf).astype(BF16)
    down_part = contract_cols(activated, down_t).astype(BF16).reshape(t3)

    slope = cdf + upper * jnp.exp(-0.5 * upper * upper) * 0.3989422804014327
    grad_act = jnp.dot(cot_g, down_t, preferred_element_type=F32)
    grad_upper = (grad_act * slope).astype(BF16)
    dc_part = contract_cols(grad_upper, up_full).astype(BF16).reshape(t3)
    down_grad_t = contract_rows(cot_g, activated)
    up_grad = contract_rows(c_g, grad_upper)
    mlp = jnp.concatenate([up_grad, down_grad_t], axis=1).astype(BF16).reshape(n, wrows, 2 * ff)
    mlp_blocks = pltpu.VMEM((half, wrows, 2 * ff), BF16)
    encoded, dh, dz_g, vec2, mlp = call(
        turn_kernel, sizes, 4,
        [((rows, D), BF16), ((rows, D), F32), (t3, BF16), ((4, D), F32),
         ((half, wrows, 2 * ff), BF16)],
        [pltpu.VMEM((t_count - 1, rows, D), BF16), pltpu.VMEM((t_count - 1, rows, D), BF16),
         pltpu.VMEM((rows, D), BF16), mlp_blocks] + [dma(t_count)] * 6 + [dma(half)] * 2,
        down_part, dc_part, hidden, out_cotangent, gains[1:2], pbias[3:4], mlp,
    )
    dz_g = dz_g.reshape(group, D)
    fc_grad = place_slice(jnp.sum(grad_upper, axis=0, dtype=F32), t_idx, ff_all)
    outs = contract_rows(dz_g, attended).astype(BF16).reshape(n, wrows, width)
    grad_attended = jnp.dot(dz_g, out_t, preferred_element_type=F32).astype(BF16)
    grad_queries, dkv_sum, mlp, out_grad = call(
        back_kernel, sizes, 5,
        [((group, width), BF16), ((group, 2 * width), F32), ((wrows, 2 * ff), F32),
         ((wrows, width), F32)],
        [pltpu.VMEM((blocks, group, group), F32)] * 2 + [pltpu.VMEM((HEAD, group), F32)]
        + [pltpu.VMEM((blocks, group, 2 * width), BF16), pltpu.VMEM((6, group, 2 * width), BF16)]
        + [mlp_blocks] + [pltpu.VMEM((half, wrows, width), BF16)] * 3
        + [dma(6)] * 2 + [dma(half)] * 6,
        queries, window, grad_attended, lse, qid, kid.reshape(blocks, group, 1), mlp, outs,
    )
    out_grad = out_grad.T
    up_grad = mlp[:, :ff]
    down_grad = mlp[:, ff:].T

    grad_proj = jnp.concatenate([grad_queries, dkv_sum.astype(BF16)], axis=1)
    qkv_grad = contract_rows(normed_g, grad_proj).astype(BF16)
    bias_sums = jnp.sum(grad_proj, axis=0, dtype=F32)
    da_part = contract_cols(grad_proj, qkv_full).astype(BF16).reshape(t3)
    zero = jnp.zeros((1, D), F32)
    vec = jnp.concatenate([
        zero, vec2[0:1], zero, vec2[1:2],
        place_slice(bias_sums[:width], t_idx, D)[None],
        place_slice(bias_sums[2 * width:], t_idx, D)[None],
        vec2[2:4], fc_grad.reshape(-1, D), zero, zero, zero, zero,
    ], axis=0)
    vshape = vec.shape
    frames_grad, qkv_grad, vec = call(
        close_kernel, sizes, 6,
        [((rows, D), BF16), ((wrows, 3 * width), F32), (vshape, F32)],
        [pltpu.VMEM((t_count - 1, rows, D), BF16)]
        + [pltpu.VMEM((half, wrows, 3 * width), BF16)] * 3
        + [pltpu.VMEM(vshape, F32), pltpu.VMEM((t_count - 1,) + vshape, F32),
           pltpu.VMEM((t_count,) + vshape, F32), pltpu.VMEM((2,) + vshape, F32),
           pltpu.VMEM(vshape, F32), pltpu.VMEM((half,) + vshape, F32)]
        + [dma(t_count)] * 2 + [dma(half)] * 4 + [dma(t_count)] * 2 + [dma(1)] * 2
        + [dma(half)] * 2,
        da_part, frames, dh, gains[0:1], qkv_grad.reshape(n, wrows, 3 * width), vec,
    )
    fc_rows = ff_all // D
    return (
        encoded,
        frames_grad,
        qkv_grad.reshape(1, wrows, 3, width),
        out_grad[None],
        up_grad[None],
        down_grad[None],
        vec[None, 0:2],
        vec[None, 2:4],
        vec[None, 4:8],
        vec[8:8 + fc_rows].reshape(1, ff_all),
    )


def solution(mesh):
    return jax.shard_map(
        shards,
        mesh=mesh,
        in_specs=(
            P(("dp", "tensor"), None),
            P(),
            P(None, "dp", None, "tensor"),
            P(None, "tensor", "dp"),
            P(None, "dp", "tensor"),
            P(None, "tensor", "dp"),
            P(),
            P(),
            P(),
            P(),
            P(("dp", "tensor"), None),
        ),
        out_specs=(
            P(("dp", "tensor"), None),
            P(("dp", "tensor"), None),
            P(None, "dp", None, "tensor"),
            P(None, "tensor", "dp"),
            P(None, "dp", "tensor"),
            P(None, "tensor", "dp"),
            P(),
            P(),
            P(),
            P(),
        ),
        check_vma=False,
    )
```
